32 devices in a mesh: gx: 4 (over y, x), yz: 8 (over z, core).
Axes of the slice: x: 2, y: 2, z: 4, core: 2. Of those that a mesh axis runs over, the one named last changes fastest.
Arguments:
- tokens: bfloat16 [4, 256, 18432], P('gx', None, 'yz'), may hold values from -6 to 6
- gain: float32 [18432], replicated, may hold values from 0.1 to 1.9
- w_query: bfloat16 [18432, 8192], P('gx', 'yz'), may hold values from -0.046875 to 0.046875
- w_keyval: bfloat16 [18432, 512], P('gx', 'yz'), may hold values from -0.09375 to 0.09375
- w_out: bfloat16 [8192, 18432], P('gx', 'yz'), may hold values from -0.375 to 0.375
- cache: bfloat16 [4, 2048, 512], P('gx', 'yz'), as said below
- lengths: int32 [4], P('gx'), may hold values from 1024 to 2048, as said below
Outputs:
- attended: bfloat16 [4, 256, 18432], P('gx', None, 'yz')
The draws below stay inside these ranges and needn't reach their ends.
Inputs may be any that keep to these rules, and one draw needn't show every extreme that they name: `lengths`: some sequence has exactly 2048 filled slots and some exactly 1024. `cache`: cached keys are already rotated to their slot positions.
All inputs are finite; a program needn't handle non-finite values.
Results may differ from the reference program's by a relative error of at most 0.012.
The reference program's roundings to bfloat16 on the way count: a program that leaves them out, or rounds other values in their place, can miss the bound.
Values may be sent and summed in bfloat16 or wider, within the bound.
No kernel may reach another device: no remote copies, remote signals or barrier semaphores. Data moves between devices by JAX's collectives and lax.ppermute only.
A program may use at most 192 MiB of HBM per device.

```python
import math
import jax
import jax.numpy as jnp
from jax import lax

D = 18432
HEAD = 256
HEADS = 32
SPAN = 256
CACHE = 2048
BATCH = 4
QWIDTH = 8192


def draw_lengths(key, part):
    key = jax.random.fold_in(key, 7)
    first, second = jax.random.split(key)
    filled = jax.random.randint(first, (BATCH,), CACHE // 2, CACHE + 1)
    order = jax.random.permutation(second, BATCH)
    filled = filled.at[order[0]].set(CACHE)
    filled = filled.at[order[1]].set(CACHE // 2)
    return filled.astype(jnp.int32)


def draw_cache(key, part):
    key = jax.random.fold_in(key, 11)
    keys_list = jax.random.split(key, 4)
    stored_keys = 2.0 * jax.random.normal(keys_list[2], (BATCH, CACHE, HEAD), jnp.float32)
    stored_values = jax.random.normal(keys_list[3], (BATCH, CACHE, HEAD), jnp.float32)
    return jnp.concatenate([stored_keys, stored_values], axis=-1).astype(jnp.bfloat16)


def shard_levels(stream_key, extent, pieces, low, high):
    level = 1.0
    for position, shards_of in pieces:
        steps = jax.random.uniform(jax.random.fold_in(jax.random.fold_in(stream_key, 6), position), (shards_of,), jnp.float32, low / len(pieces), high / len(pieces))
        level = level * jnp.repeat(jnp.exp(steps), extent[position] // shards_of).reshape((-1,) + (1,) * (len(extent) - 1 - position))
    return level


def centred(own_key, extent, deviation, limit, shards=(), held_as=jnp.bfloat16):
    entries = deviation * jax.random.normal(own_key, extent, jnp.float32)
    if shards:
        entries = entries * shard_levels(own_key, extent, shards, -0.22, 0.18)
    return jnp.clip(entries, -limit, limit).astype(held_as)


def setup_inputs(seed: int = 0) -> dict:
    splits = jax.random.split(jax.random.key(seed), 8)
    return {
        "tokens": centred(splits[0], (BATCH, SPAN, D), 1.0, 6.0, ((0, 4), (2, 8))),
        "gain": jnp.clip(1.0 + 0.18 * jax.random.normal(splits[1], (D,), jnp.float32), 0.1, 1.9),
        "w_query": centred(splits[2], (D, QWIDTH), D ** -0.5, 0.046875, ((0, 4), (1, 8))),
        "w_keyval": centred(splits[3], (D, 2 * HEAD), (D // 4) ** -0.5, 0.09375, ((0, 4), (1, 8))),
        "w_out": centred(splits[4], (QWIDTH, D), HEAD ** -0.5, 0.375, ((0, 4), (1, 8))),
        "cache": draw_cache(jax.random.fold_in(splits[7], 71), 0),
        "lengths": draw_lengths(jax.random.fold_in(splits[7], 71), 0),
    }


def layer_norm(tokens, gain):
    values = tokens.astype(jnp.float32)
    mean = lax.optimization_barrier(jnp.mean(values, axis=-1, keepdims=True))
    centered = values - mean
    spread = lax.optimization_barrier(jnp.mean(centered * centered, axis=-1, keepdims=True))
    return (centered * lax.rsqrt(spread + 1e-06) * gain).astype(jnp.bfloat16)

def rotate(values, positions):
    width = values.shape[-1]
    half = width // 2
    freq = jnp.exp(jnp.arange(half, dtype=jnp.float32) * (-2.0 * math.log(10000.0) / width))
    angles = positions.astype(jnp.float32)[..., None] * freq
    cosine = jnp.cos(angles)[:, :, None, :]
    sine = jnp.sin(angles)[:, :, None, :]
    first = values[..., :half]
    second = values[..., half:]
    return jnp.concatenate([first * cosine - second * sine, second * cosine + first * sine], axis=-1)

def reference(tokens, gain, w_query, w_keyval, w_out, cache, lengths):
    normed = layer_norm(tokens, gain)
    flat = normed.reshape(BATCH * SPAN, D)
    positions = lengths[:, None] + jnp.arange(SPAN, dtype=jnp.int32)[None, :]
    query_raw = jnp.dot(flat, w_query, preferred_element_type=jnp.float32).reshape(BATCH, SPAN, HEADS, HEAD)
    query = rotate(query_raw, positions).astype(jnp.bfloat16)
    keyval = jnp.dot(flat, w_keyval, preferred_element_type=jnp.float32).astype(jnp.bfloat16).reshape(BATCH, SPAN, 2 * HEAD)
    fresh_keys = rotate(keyval[:, :, None, :HEAD].astype(jnp.float32), positions)[:, :, 0, :].astype(jnp.bfloat16)
    fresh_values = keyval[:, :, HEAD:]
    keys_all = jnp.concatenate([cache[:, :, :HEAD], fresh_keys], axis=1)
    values_all = jnp.concatenate([cache[:, :, HEAD:], fresh_values], axis=1)
    slots = jnp.arange(CACHE + SPAN, dtype=jnp.int32)
    steps = jnp.arange(SPAN, dtype=jnp.int32)
    cached_ok = (slots[None, None, :] < lengths[:, None, None]) & (slots[None, None, :] < CACHE)
    fresh_ok = (slots[None, None, :] >= CACHE) & (slots[None, None, :] - CACHE <= steps[None, :, None])
    valid = cached_ok | fresh_ok
    scale = 1.0 / math.sqrt(HEAD)

    def one_head(index):
        row = index // HEADS
        which = index % HEADS
        asked = query[row][:, which, :]
        scores = jnp.dot(asked, keys_all[row].T, preferred_element_type=jnp.float32) * scale
        mask = valid[row]
        largest = lax.optimization_barrier(jnp.max(jnp.where(mask, scores, -1e+30), axis=-1, keepdims=True))
        probs = jnp.exp(jnp.where(mask, scores - largest, -jnp.inf))
        total = lax.optimization_barrier(jnp.sum(probs, axis=-1, keepdims=True))
        summed = jnp.dot(probs.astype(jnp.bfloat16), values_all[row], preferred_element_type=jnp.float32)
        return (summed / total).astype(jnp.bfloat16)
    outputs = lax.map(one_head, jnp.arange(BATCH * HEADS, dtype=jnp.int32))
    outputs = outputs.reshape(BATCH, HEADS, SPAN, HEAD).transpose(0, 2, 1, 3).reshape(BATCH * SPAN, QWIDTH)
    attended = jnp.dot(outputs, w_out, preferred_element_type=jnp.float32).astype(jnp.bfloat16)
    return attended.reshape(BATCH, SPAN, D)
```

```python
import functools
import math

import jax
import jax.numpy as jnp
from jax import lax
from jax.experimental import pallas as pl
from jax.experimental.pallas import tpu as pltpu
from jax.sharding import PartitionSpec as P

HEAD = 256
HALF = HEAD // 2
SHARES = (4, 4)
VMEM = 26 << 20
FREE = pl.CostEstimate(flops=0, bytes_accessed=0, transcendentals=0)


def in_hbm(array):
    return pltpu.with_memory_space_constraint(array, pltpu.HBM)


def pick_kernel(parts, index, *refs):
    held, outs, sems = refs[:parts], refs[parts:-1], refs[-1]
    for k, out in enumerate(outs):
        for m, block in enumerate(held):

            @pl.when(index[k] == m)
            def _():
                pltpu.make_async_copy(block, out, sems.at[k]).start()

    for k, out in enumerate(outs):
        pltpu.make_async_copy(held[0], out, sems.at[k]).wait()


def pick(index, held):
    parts = len(held)
    block = held[0]
    return pl.pallas_call(
        functools.partial(pick_kernel, parts),
        grid_spec=pltpu.PrefetchScalarGridSpec(
            num_scalar_prefetch=1,
            grid=(),
            in_specs=[pl.BlockSpec(memory_space=pl.ANY)] * parts,
            out_specs=[pl.BlockSpec(memory_space=pl.ANY)] * parts,
            scratch_shapes=[pltpu.SemaphoreType.DMA((parts,))],
        ),
        out_shape=[jax.ShapeDtypeStruct(block.shape, block.dtype)] * parts,
        compiler_params=pltpu.CompilerParams(vmem_limit_bytes=VMEM),
        cost_estimate=FREE,
    )(index, *held)


def normalise_kernel(parts, index, mean, factor, gains, *refs):
    outs, held, blocks, sems = refs[-2 - parts : -2], refs[: -2 - parts], refs[-2], refs[-1]
    for k in range(parts):
        for m, block in enumerate(held):

            @pl.when(index[k] == m)
            def _():
                pltpu.make_async_copy(block, blocks.at[k], sems.at[k]).start()

    for k, out in enumerate(outs):
        pltpu.make_async_copy(held[0], blocks.at[k], sems.at[k]).wait()
        gain = gains[k : k + 1, :]

        @pl.loop(0, out.shape[0], step=32)
        def _(start):
            rows = pl.ds(pl.multiple_of(start, 32), 32)
            centred = blocks[k, rows, :].astype(jnp.float32) - mean[rows, :]
            out[rows, :] = (centred * factor[rows, :] * gain).astype(out.dtype)


def normalise(index, mean, factor, gains, held):
    parts = index.shape[0]
    block = held[0]
    inside = pl.BlockSpec(memory_space=pltpu.VMEM)
    return pl.pallas_call(
        functools.partial(normalise_kernel, parts),
        grid_spec=pltpu.PrefetchScalarGridSpec(
            num_scalar_prefetch=1,
            grid=(),
            in_specs=[inside] * 3 + [pl.BlockSpec(memory_space=pl.ANY)] * len(held),
            out_specs=[inside] * parts,
            scratch_shapes=[
                pltpu.VMEM((parts, *block.shape), block.dtype),
                pltpu.SemaphoreType.DMA((parts,)),
            ],
        ),
        out_shape=[jax.ShapeDtypeStruct(block.shape, block.dtype)] * parts,
        compiler_params=pltpu.CompilerParams(vmem_limit_bytes=VMEM),
        cost_estimate=FREE,
    )(index, mean, factor, gains, *held)


def join_kernel(*refs):
    *pieces, out, sems = refs
    size = pieces[0].shape[0]
    copies = [
        pltpu.make_async_copy(piece, out.at[pl.ds(i * size, size)], sems.at[i])
        for i, piece in enumerate(pieces)
    ]
    for copy in copies:
        copy.start()
    for copy in copies:
        copy.wait()


def join(pieces):
    size, columns = pieces[0].shape
    return pl.pallas_call(
        join_kernel,
        in_specs=[pl.BlockSpec(memory_space=pl.ANY)] * len(pieces),
        out_specs=pl.BlockSpec(memory_space=pl.ANY),
        scratch_shapes=[pltpu.SemaphoreType.DMA((len(pieces),))],
        out_shape=jax.ShapeDtypeStruct((len(pieces) * size, columns), pieces[0].dtype),
        compiler_params=pltpu.CompilerParams(vmem_limit_bytes=VMEM),
        cost_estimate=FREE,
    )(*pieces)


def tail_kernel(*refs):
    *parts, out = refs
    total = parts[0][...]
    for part in parts[1:]:
        total += part[...].astype(jnp.float32)
    out[...] = total.astype(out.dtype)


def tail_sum(parts, columns):
    size, total = parts[0].shape
    last = total // columns - 1
    return pl.pallas_call(
        tail_kernel,
        grid=(1,),
        in_specs=[pl.BlockSpec((size, columns), lambda i: (0, last))] * len(parts),
        out_specs=pl.BlockSpec((size, columns), lambda i: (0, 0)),
        out_shape=jax.ShapeDtypeStruct((size, columns), jnp.bfloat16),
        compiler_params=pltpu.CompilerParams(vmem_limit_bytes=VMEM),
        cost_estimate=FREE,
    )(*parts)


def widest(columns):
    for width in (768, 512, 256):
        if columns % width == 0:
            return width
    return columns


def product_kernel(groups, joined, which, *refs):
    near_pieces, far_pieces, refs = refs[:groups], refs[groups : groups + joined], refs[groups + joined :]
    weight, refs = refs[0], refs[1:]
    extra, narrow = None, None
    if len(refs) > groups + 4:
        extra, narrow, refs = refs[:2], refs[-1], refs[2:-1]
    outs, (rows, tiles, sums, sems) = refs[:groups], refs[groups:]
    blocks, _, deep = rows.shape
    size, depth = near_pieces[0].shape
    columns = weight.shape[1]
    shares = blocks // 2
    width = widest(columns)

    waits = []
    for block in range(blocks):
        half, share = block // shares, block % shares
        mine = half == 0
        row = pl.multiple_of((which[0] if mine else 1 - which[0]) * depth + share * deep, deep)
        part = slice(share * deep, (share + 1) * deep)
        pieces = near_pieces if mine else far_pieces
        tall = groups * size // len(pieces)
        moves = [
            (piece.at[:, part], rows.at[block, pl.ds(i * tall, tall)]) for i, piece in enumerate(pieces)
        ]
        moves.append((weight.at[pl.ds(row, deep)], tiles.at[block]))
        if extra is not None:
            for other, source in enumerate(extra):
                high = source.shape[0]
                place = which[0] if other == 0 else 1 - which[0]
                moves.append(
                    (
                        source.at[:, pl.ds(row, deep)],
                        narrow.at[block, pl.ds(pl.multiple_of(place * high, high), high)],
                    )
                )
        waits.append(
            [pltpu.make_async_copy(a, b, sems.at[block, i]) for i, (a, b) in enumerate(moves)]
        )
    for copies in waits:
        for copy in copies:
            copy.start()

    def add(total, place, block):
        if block:
            total += sums[:, place]
        if block < blocks - 1:
            sums[:, place] = total
        else:
            for k, out in enumerate(outs):
                out[:, place] = total[k * size : (k + 1) * size].astype(out.dtype)

    for block, copies in enumerate(waits):
        for copy in copies:
            copy.wait()
        if extra is not None:
            total = lax.dot_general(
                rows[block], narrow[block], (((1,), (1,)), ((), ())), preferred_element_type=jnp.float32
            )
            add(total, slice(columns, None), block)

        @pl.loop(0, columns // width)
        def _(j):
            place = pl.ds(pl.multiple_of(j * width, width), width)
            total = jnp.dot(rows[block], tiles[block, :, place], preferred_element_type=jnp.float32)
            add(total, place, block)


def product(which, own, other, weight, extra=None):
    groups = len(own)
    size, depth = own[0].shape
    columns = weight.shape[1]
    shares = 2 if depth % 256 == 0 and depth > 1024 else 1
    deep = depth // shares
    weights = [weight]
    total = columns
    if extra is not None:
        weights += extra
        total += 2 * extra[0].shape[0]
    scratch = [
        pltpu.VMEM((2 * shares, groups * size, deep), jnp.bfloat16),
        pltpu.VMEM((2 * shares, deep, columns), jnp.bfloat16),
        pltpu.VMEM((groups * size, total), jnp.float32),
        pltpu.SemaphoreType.DMA((2 * shares, groups + 3)),
    ]
    if extra is not None:
        scratch.append(pltpu.VMEM((2 * shares, total - columns, deep), jnp.bfloat16))
    operands = [*own, *other, *map(in_hbm, weights)]
    return pl.pallas_call(
        functools.partial(product_kernel, groups, len(other)),
        grid_spec=pltpu.PrefetchScalarGridSpec(
            num_scalar_prefetch=1,
            grid=(),
            in_specs=[pl.BlockSpec(memory_space=pl.ANY)] * len(operands),
            out_specs=[pl.BlockSpec(memory_space=pltpu.VMEM)] * groups,
            scratch_shapes=scratch,
        ),
        out_shape=[
            jax.ShapeDtypeStruct((size, total), jnp.bfloat16 if k else jnp.float32) for k in range(groups)
        ],
        compiler_params=pltpu.CompilerParams(vmem_limit_bytes=VMEM),
        cost_estimate=FREE,
    )(which, *operands)


def attend_kernel(sizes, heads, parts, info, *refs):
    chunk = len(sizes) - 1
    size = sizes[-1]
    starts = [sum(sizes[:c]) for c in range(len(sizes))]
    count = parts + 3 + parts * (chunk + 1)
    sources, out, held = refs[:count], refs[count], refs[count + 1 : -3]
    keys, values, sems = refs[-3:]
    queries, held = held[:parts], held[parts:]
    cosine, sine, past = held[:3]
    pairs = held[3:]
    length = info[0]
    z = info[1]
    step = pl.program_id(0)

    def turned(first, second, rows):
        cos = cosine[rows, :]
        sin = sine[rows, :]
        return first * cos - second * sin, second * cos + first * sin

    @pl.when(step == 0)
    def _():
        copies = [
            pltpu.make_async_copy(source, target, sems.at[i])
            for i, (source, target) in enumerate(zip(sources, refs[count + 1 : -3]))
        ]
        for copy in copies:
            copy.start()
        for copy in copies:
            copy.wait()
        for c in range(chunk + 1):
            rows = slice(starts[c], starts[c] + sizes[c])
            found = []
            for a in range(parts):
                block = pairs[c * parts][...]
                for k in range(1, parts):
                    block = jnp.where(z == a ^ k, pairs[c * parts + k][...], block)
                found.append(block)
            joined = jnp.concatenate(found, axis=1)
            first, second = turned(
                joined[:, :HALF].astype(jnp.float32), joined[:, HALF:HEAD].astype(jnp.float32), rows
            )
            keys[rows, :HALF] = first.astype(jnp.bfloat16)
            keys[rows, HALF:] = second.astype(jnp.bfloat16)
            values[rows, :] = joined[:, HEAD:]

    here = pl.ds(pl.multiple_of(step * (heads * HEAD), heads * HEAD), heads * HEAD)
    raw = queries[0][:, here]
    for k in range(1, parts):
        raw = raw + queries[k][:, here].astype(jnp.float32)
    asked = []
    for h in range(heads):
        first, second = turned(
            raw[:, h * HEAD : h * HEAD + HALF],
            raw[:, h * HEAD + HALF : (h + 1) * HEAD],
            slice(starts[-1], starts[-1] + size),
        )
        asked.append(jnp.concatenate([first.astype(jnp.bfloat16), second.astype(jnp.bfloat16)], axis=1))
    query = jnp.concatenate(asked, axis=0)
    scale = 1.0 / math.sqrt(HEAD)
    dims = (((1,), (1,)), ((), ()))
    old = lax.dot_general(query, past[:, :HEAD], dims, preferred_element_type=jnp.float32) * scale
    new = lax.dot_general(query, keys[...], dims, preferred_element_type=jnp.float32) * scale
    slot = lax.broadcasted_iota(jnp.int32, (1, old.shape[1]), 1)
    old = jnp.where(slot < length, old, -jnp.inf)
    row = lax.broadcasted_iota(jnp.int32, new.shape, 0) % size + starts[-1]
    column = lax.broadcasted_iota(jnp.int32, new.shape, 1)
    new = jnp.where(column <= row, new, -jnp.inf)
    top = jnp.maximum(jnp.max(old, axis=1, keepdims=True), jnp.max(new, axis=1, keepdims=True))
    old = jnp.exp(old - top)
    new = jnp.exp(new - top)
    total = jnp.sum(old, axis=1, keepdims=True) + jnp.sum(new, axis=1, keepdims=True)
    summed = jnp.dot(old.astype(jnp.bfloat16), past[:, HEAD:], preferred_element_type=jnp.float32)
    summed += jnp.dot(new.astype(jnp.bfloat16), values[...], preferred_element_type=jnp.float32)
    result = (summed / total).astype(jnp.bfloat16)
    for h in range(heads):
        out[:, h * HEAD : (h + 1) * HEAD] = result[h * size : (h + 1) * size]


def attend(info, queries, cosine, sine, past, pairs):
    parts = len(queries)
    size = queries[0].shape[0]
    columns = queries[0].shape[1] - pairs[0][0].shape[1]
    heads = columns // HEAD
    at_once = 2 if heads % 2 == 0 else 1
    operands = [*queries, cosine, sine, past, *[p for group in pairs for p in group]]
    sizes = tuple(group[0].shape[0] for group in pairs)
    fresh = sum(sizes)
    return pl.pallas_call(
        functools.partial(attend_kernel, sizes, at_once, parts),
        grid_spec=pltpu.PrefetchScalarGridSpec(
            num_scalar_prefetch=1,
            grid=(heads // at_once,),
            in_specs=[pl.BlockSpec(memory_space=pl.ANY)] * len(operands),
            out_specs=pl.BlockSpec((size, at_once * HEAD), lambda h, w: (0, h)),
            scratch_shapes=[pltpu.VMEM(a.shape, a.dtype) for a in operands]
            + [
                pltpu.VMEM((fresh, HEAD), jnp.bfloat16),
                pltpu.VMEM((fresh, HEAD), jnp.bfloat16),
                pltpu.SemaphoreType.DMA((len(operands),)),
            ],
        ),
        out_shape=jax.ShapeDtypeStruct((size, columns), jnp.bfloat16),
        compiler_params=pltpu.CompilerParams(vmem_limit_bytes=VMEM),
        cost_estimate=FREE,
    )(info, *queries, *map(in_hbm, operands[parts : parts + 3]), *operands[parts + 3 :])


def solution(mesh):
    n_gx = mesh.shape["gx"]
    n_yz = mesh.shape["yz"]
    inner = n_yz // n_gx
    groups = [[z * inner + r for r in range(inner)] for z in range(n_gx)]
    swap = [(j, j ^ 1) for j in range(n_yz)]

    def tie(value, earlier):
        return lax.optimization_barrier((value, earlier))[0]

    def hop(block, k):
        pairs = [(a * inner + b, (a ^ k) * inner + b) for a in range(n_gx) for b in range(inner)]
        return lax.ppermute(block, "yz", pairs)

    def around(block, end=n_gx):
        return complete([block], end)

    def complete(held, end=n_gx):
        held = list(held)
        for m in range(len(held), end):
            low = m & -m
            block = held[m - low]
            held.append(hop(tie(block, held[1:m]) if m != low else block, low))
        return held

    def turn(picks):
        return [exchange(block, k) for k, block in enumerate(picks)]

    def exchange(block, k):
        if k == 0:
            return block
        return lax.ppermute(block, "gx", [(s, s ^ k) for s in range(n_gx)])

    def times(rows, other, which, weight, extra=None):
        if inner == 2:
            return product(which, rows, other, weight, extra)
        if extra is not None:
            weight = jnp.concatenate([weight, extra], axis=1)
        out = jnp.dot(other, weight, preferred_element_type=jnp.float32)
        out = out.reshape(n_gx, -1, weight.shape[1])
        return [out[0]] + [out[k].astype(jnp.bfloat16) for k in range(1, n_gx)]

    def partner(rows, joined):
        if inner == 2:
            if joined == 1:
                rows = [tie(rows[0], rows[1]), *rows[1:]]
            else:
                rows = [join(rows[i : i + joined]) for i in range(0, n_gx, joined)]
            return [lax.ppermute(block, "yz", swap) for block in rows]
        rows = jnp.concatenate(rows, axis=0)
        return lax.all_gather(rows, "yz", axis=1, tiled=True, axis_index_groups=groups)

    def give(partial):
        return [exchange(p, k) for k, p in enumerate(partial)]

    def collect(partial):
        total = partial[0]
        for p in partial[1:]:
            total = total + p.astype(jnp.float32)
        return total.astype(jnp.bfloat16)

    def pair_columns(part, r):
        if inner == 2:
            other = lax.ppermute(part, "yz", swap)
            return jnp.concatenate(
                [jnp.where(r == 0, part, other), jnp.where(r == 0, other, part)], axis=1
            )
        return lax.all_gather(part, "yz", axis=1, tiled=True, axis_index_groups=groups)

    def across(part):
        return [part] + [hop(part, k) for k in range(1, n_gx)]

    def body(tokens, gain, w_query, w_keyval, w_out, cache, lengths):
        gx = lax.axis_index("gx")
        yz = lax.axis_index("yz")
        z = yz // inner
        r = yz % inner
        _, span, width = tokens.shape
        features = width * n_yz
        n_yz_columns = w_keyval.shape[1]
        ends = [span * sum(SHARES[: t + 1]) // sum(SHARES) for t in range(len(SHARES))]
        parts = [slice(start, end) for start, end in zip([0] + ends, ends)]
        length = lengths[0]

        first = around(tokens[0, parts[0]])

        values = tokens[0].astype(jnp.float32)
        mine = jnp.mean(values, axis=-1)
        moment = jnp.sum(jnp.square(values - mine[:, None]), axis=-1)
        stats = pair_columns(jnp.stack([mine, moment])[:, None], r)
        stats = jnp.concatenate(across(stats), axis=1)
        mean = jnp.mean(stats[0], axis=0)
        moments = jnp.sum(stats[1], axis=0) + width * jnp.sum(
            jnp.square(stats[0] - mean), axis=0
        )
        factor = lax.rsqrt(moments / features + 1e-06)
        gains = gain.reshape(n_gx, inner, width)[gx ^ jnp.arange(n_gx), r]
        if inner == 2:
            w_keyval = w_keyval.T
            w_keyval = [w_keyval, lax.ppermute(tie(w_keyval, first[3]), "yz", swap)]
        else:
            w_keyval = pair_columns(w_keyval, r)

        which = r[None]
        info = jnp.stack([length, z])
        freq = jnp.exp(jnp.arange(HALF, dtype=jnp.float32) * (-2.0 * math.log(10000.0) / HEAD))
        positions = length + jnp.arange(span, dtype=jnp.int32)
        angles = positions.astype(jnp.float32)[:, None] * freq
        cosine = jnp.cos(angles)
        sine = jnp.sin(angles)

        index = z ^ gx ^ jnp.arange(n_gx, dtype=jnp.int32)
        order = [range(1, n_gx - 1), [n_gx - 1, 0]]
        shares = [
            (jnp.stack([z ^ gx ^ k for k in ks]), jnp.stack([gains[k] for k in ks])) for ks in order
        ]
        mean, factor, shares = tie(
            (mean[:, None], factor[:, None], shares), (cosine, sine, info, which, index)
        )

        def normalised(t, held, earlier=()):
            picks = {}
            for ks, (some, scale) in zip(order, shares):
                blocks = normalise(some, mean[parts[t]], factor[parts[t]], scale, held)
                picks.update(zip(ks, blocks))
                held = tie(held, (blocks, earlier))
            return [picks[k] for k in range(n_gx)]

        pairs = []

        def fresh(queries):
            columns = inner * n_yz_columns
            return across(tail_sum(queries, columns))

        second = around(tie(tokens[0, parts[1]], first[3]))
        rows = turn(normalised(0, first))
        past = lax.all_gather(tie(cache, (second[1:3], rows[1:])), "yz", axis=1, tiled=True)[0]
        rows[-1] = tie(rows[-1], second[1:3])
        partial = times(rows, partner(rows, 1), which, w_query, w_keyval)
        queries = give(partial)
        pairs.append(fresh(queries))

        picks = normalised(1, tie(second, partial[0]), queries)
        rows = turn(picks)
        heads = attend(info, tie(queries, picks[0]), cosine, sine, past, pairs)
        first = around(heads)

        rows = tie(rows, first[1:3])
        other = partner(rows, 2)
        picks = pick(index, first)
        first_rows = turn(picks)
        rows, other = tie((rows, other), picks)
        partial = times(rows, other, which, w_query, w_keyval)
        queries = give(partial)

        rows = tie(first_rows, partial[0])
        partial = times(rows, partner(rows, 4), which, w_out)
        outs = [give(partial)]

        queries = tie(queries, partial[0])
        pairs.append(fresh(queries))
        heads = attend(info, queries, cosine, sine, past, pairs)
        rows = turn(pick(index, tie(around(heads), outs[0][1:])))
        outs.append(give(times(rows, partner(rows, 4), which, w_out)))
        outs = [collect(o) for o in outs]
        return jnp.concatenate(outs, axis=0)[None]

    return jax.shard_map(
        body,
        mesh=mesh,
        in_specs=(
            P("gx", None, "yz"),
            P(),
            P("gx", "yz"),
            P("gx", "yz"),
            P("gx", "yz"),
            P("gx", "yz", None),
            P("gx"),
        ),
        out_specs=P("gx", None, "yz"),
        check_vma=False,
    )
```

```python
import functools
import math

import jax
import jax.numpy as jnp
from jax import lax
from jax.experimental import pallas as pl
from jax.experimental.pallas import tpu as pltpu
from jax.sharding import PartitionSpec as P

HEAD = 256
HALF = HEAD // 2
SHARES = (4, 4)
VMEM = 26 << 20
STRIPS = 4
FREE = pl.CostEstimate(flops=0, bytes_accessed=0, transcendentals=0)


def in_hbm(array):
    return pltpu.with_memory_space_constraint(array, pltpu.HBM)


def pick_kernel(parts, index, *refs):
    held, outs, sems = refs[:parts], refs[parts:-1], refs[-1]
    for k, out in enumerate(outs):
        for m, block in enumerate(held):

            @pl.when(index[k] == m)
            def _():
                pltpu.make_async_copy(block, out, sems.at[k]).start()

    for k, out in enumerate(outs):
        pltpu.make_async_copy(held[0], out, sems.at[k]).wait()


def pick(index, held):
    parts = len(held)
    block = held[0]
    return pl.pallas_call(
        functools.partial(pick_kernel, parts),
        grid_spec=pltpu.PrefetchScalarGridSpec(
            num_scalar_prefetch=1,
            grid=(),
            in_specs=[pl.BlockSpec(memory_space=pl.ANY)] * parts,
            out_specs=[pl.BlockSpec(memory_space=pl.ANY)] * parts,
            scratch_shapes=[pltpu.SemaphoreType.DMA((parts,))],
        ),
        out_shape=[jax.ShapeDtypeStruct(block.shape, block.dtype)] * parts,
        compiler_params=pltpu.CompilerParams(vmem_limit_bytes=VMEM),
        cost_estimate=FREE,
    )(index, *held)


def normalise_kernel(parts, index, mean, factor, gains, *refs):
    outs, held, blocks, sems = refs[-2 - parts : -2], refs[: -2 - parts], refs[-2], refs[-1]
    for k in range(parts):
        for m, block in enumerate(held):

            @pl.when(index[k] == m)
            def _():
                pltpu.make_async_copy(block, blocks.at[k], sems.at[k]).start()

    for k, out in enumerate(outs):
        pltpu.make_async_copy(held[0], blocks.at[k], sems.at[k]).wait()
        gain = gains[k : k + 1, :]

        @pl.loop(0, out.shape[0], step=32)
        def _(start):
            rows = pl.ds(pl.multiple_of(start, 32), 32)
            centred = blocks[k, rows, :].astype(jnp.float32) - mean[rows, :]
            out[rows, :] = (centred * factor[rows, :] * gain).astype(out.dtype)


def normalise(index, mean, factor, gains, held):
    parts = index.shape[0]
    block = held[0]
    inside = pl.BlockSpec(memory_space=pltpu.VMEM)
    return pl.pallas_call(
        functools.partial(normalise_kernel, parts),
        grid_spec=pltpu.PrefetchScalarGridSpec(
            num_scalar_prefetch=1,
            grid=(),
            in_specs=[inside] * 3 + [pl.BlockSpec(memory_space=pl.ANY)] * len(held),
            out_specs=[inside] * parts,
            scratch_shapes=[
                pltpu.VMEM((parts, *block.shape), block.dtype),
                pltpu.SemaphoreType.DMA((parts,)),
            ],
        ),
        out_shape=[jax.ShapeDtypeStruct(block.shape, block.dtype)] * parts,
        compiler_params=pltpu.CompilerParams(vmem_limit_bytes=VMEM),
        cost_estimate=FREE,
    )(index, mean, factor, gains, *held)


def join_kernel(*refs):
    *pieces, out, sems = refs
    size = pieces[0].shape[0]
    copies = [
        pltpu.make_async_copy(piece, out.at[pl.ds(i * size, size)], sems.at[i])
        for i, piece in enumerate(pieces)
    ]
    for copy in copies:
        copy.start()
    for copy in copies:
        copy.wait()


def join(pieces):
    size, columns = pieces[0].shape
    return pl.pallas_call(
        join_kernel,
        in_specs=[pl.BlockSpec(memory_space=pl.ANY)] * len(pieces),
        out_specs=pl.BlockSpec(memory_space=pl.ANY),
        scratch_shapes=[pltpu.SemaphoreType.DMA((len(pieces),))],
        out_shape=jax.ShapeDtypeStruct((len(pieces) * size, columns), pieces[0].dtype),
        compiler_params=pltpu.CompilerParams(vmem_limit_bytes=VMEM),
        cost_estimate=FREE,
    )(*pieces)


def tail_kernel(*refs):
    *parts, out = refs
    total = parts[0][...]
    for part in parts[1:]:
        total += part[...].astype(jnp.float32)
    out[...] = total.astype(out.dtype)


def tail_sum(parts, columns):
    size, total = parts[0].shape
    last = total // columns - 1
    return pl.pallas_call(
        tail_kernel,
        grid=(1,),
        in_specs=[pl.BlockSpec((size, columns), lambda i: (0, last))] * len(parts),
        out_specs=pl.BlockSpec((size, columns), lambda i: (0, 0)),
        out_shape=jax.ShapeDtypeStruct((size, columns), jnp.bfloat16),
        compiler_params=pltpu.CompilerParams(vmem_limit_bytes=VMEM),
        cost_estimate=FREE,
    )(*parts)


def widest(columns):
    for width in (768, 512, 256):
        if columns % width == 0:
            return width
    return columns


def product_kernel(groups, joined, which, *refs):
    near_pieces, far_pieces, refs = refs[:groups], refs[groups : groups + joined], refs[groups + joined :]
    weight, refs = refs[0], refs[1:]
    extra, narrow = None, None
    if len(refs) > groups + 4:
        extra, narrow, refs = refs[:2], refs[-1], refs[2:-1]
    outs, (rows, tiles, sums, sems) = refs[:groups], refs[groups:]
    blocks, _, deep = rows.shape
    size, depth = near_pieces[0].shape
    columns = weight.shape[1]
    shares = blocks // 2
    width = widest(columns)

    waits = []
    for block in range(blocks):
        half, share = block // shares, block % shares
        mine = half == 0
        row = pl.multiple_of((which[0] if mine else 1 - which[0]) * depth + share * deep, deep)
        part = slice(share * deep, (share + 1) * deep)
        pieces = near_pieces if mine else far_pieces
        tall = groups * size // len(pieces)
        moves = [
            (piece.at[:, part], rows.at[block, pl.ds(i * tall, tall)]) for i, piece in enumerate(pieces)
        ]
        strip = deep // STRIPS
        for i in range(STRIPS):
            moves.append(
                (
                    weight.at[pl.ds(pl.multiple_of(row + i * strip, strip), strip)],
                    tiles.at[block, pl.ds(i * strip, strip)],
                )
            )
        if extra is not None:
            for other, source in enumerate(extra):
                high = source.shape[0]
                place = which[0] if other == 0 else 1 - which[0]
                moves.append(
                    (
                        source.at[:, pl.ds(row, deep)],
                        narrow.at[block, pl.ds(pl.multiple_of(place * high, high), high)],
                    )
                )
        waits.append(
            [pltpu.make_async_copy(a, b, sems.at[block, i]) for i, (a, b) in enumerate(moves)]
        )
    for copy in waits[0] + waits[1]:
        copy.start()

    def add(total, place, block):
        if block:
            total += sums[:, place]
        if block < blocks - 1:
            sums[:, place] = total
        else:
            for k, out in enumerate(outs):
                out[:, place] = total[k * size : (k + 1) * size].astype(out.dtype)

    for block, copies in enumerate(waits):
        for copy in copies:
            copy.wait()
        if block + 2 < blocks:
            for copy in waits[block + 2]:
                copy.start()
        if extra is not None:
            total = lax.dot_general(
                rows[block], narrow[block], (((1,), (1,)), ((), ())), preferred_element_type=jnp.float32
            )
            add(total, slice(columns, None), block)

        @pl.loop(0, columns // width)
        def _(j):
            place = pl.ds(pl.multiple_of(j * width, width), width)
            total = jnp.dot(rows[block], tiles[block, :, place], preferred_element_type=jnp.float32)
            add(total, place, block)


def product(which, own, other, weight, extra=None, far=False):
    groups = len(own)
    size, depth = own[0].shape
    columns = weight.shape[1]
    shares = 2 if depth % 256 == 0 and depth > 1024 else 1
    deep = depth // shares
    weights = [weight]
    total = columns
    if extra is not None:
        weights += extra
        total += 2 * extra[0].shape[0]
    scratch = [
        pltpu.VMEM((2 * shares, groups * size, deep), jnp.bfloat16),
        pltpu.VMEM((2 * shares, deep, columns), jnp.bfloat16),
        pltpu.VMEM((groups * size, total), jnp.float32),
        pltpu.SemaphoreType.DMA((2 * shares, groups + STRIPS + 2)),
    ]
    if extra is not None:
        scratch.append(pltpu.VMEM((2 * shares, total - columns, deep), jnp.bfloat16))
    if far:
        own = map(in_hbm, own)
    operands = [*own, *other, *map(in_hbm, weights)]
    return pl.pallas_call(
        functools.partial(product_kernel, groups, len(other)),
        grid_spec=pltpu.PrefetchScalarGridSpec(
            num_scalar_prefetch=1,
            grid=(),
            in_specs=[pl.BlockSpec(memory_space=pl.ANY)] * len(operands),
            out_specs=[pl.BlockSpec(memory_space=pltpu.VMEM)] * groups,
            scratch_shapes=scratch,
        ),
        out_shape=[
            jax.ShapeDtypeStruct((size, total), jnp.bfloat16 if k else jnp.float32) for k in range(groups)
        ],
        compiler_params=pltpu.CompilerParams(vmem_limit_bytes=VMEM),
        cost_estimate=FREE,
    )(which, *operands)


def attend_kernel(sizes, heads, parts, info, *refs):
    chunk = len(sizes) - 1
    size = sizes[-1]
    starts = [sum(sizes[:c]) for c in range(len(sizes))]
    count = parts + 3 + parts * (chunk + 1)
    sources, out, held = refs[:count], refs[count], refs[count + 1 : -3]
    keys, values, sems = refs[-3:]
    queries, held = held[:parts], held[parts:]
    cosine, sine, past = held[:3]
    pairs = held[3:]
    length = info[0]
    z = info[1]
    step = pl.program_id(0)

    def turned(first, second, rows):
        cos = cosine[rows, :]
        sin = sine[rows, :]
        return first * cos - second * sin, second * cos + first * sin

    @pl.when(step == 0)
    def _():
        copies = [
            pltpu.make_async_copy(source, target, sems.at[i])
            for i, (source, target) in enumerate(zip(sources, refs[count + 1 : -3]))
        ]
        for copy in copies:
            copy.start()
        for copy in copies:
            copy.wait()
        for c in range(chunk + 1):
            rows = slice(starts[c], starts[c] + sizes[c])
            found = []
            for a in range(parts):
                block = pairs[c * parts][...]
                for k in range(1, parts):
                    block = jnp.where(z == a ^ k, pairs[c * parts + k][...], block)
                found.append(block)
            joined = jnp.concatenate(found, axis=1)
            first, second = turned(
                joined[:, :HALF].astype(jnp.float32), joined[:, HALF:HEAD].astype(jnp.float32), rows
            )
            keys[rows, :HALF] = first.astype(jnp.bfloat16)
            keys[rows, HALF:] = second.astype(jnp.bfloat16)
            values[rows, :] = joined[:, HEAD:]

    here = pl.ds(pl.multiple_of(step * (heads * HEAD), heads * HEAD), heads * HEAD)
    raw = queries[0][:, here]
    for k in range(1, parts):
        raw = raw + queries[k][:, here].astype(jnp.float32)
    asked = []
    for h in range(heads):
        first, second = turned(
            raw[:, h * HEAD : h * HEAD + HALF],
            raw[:, h * HEAD + HALF : (h + 1) * HEAD],
            slice(starts[-1], starts[-1] + size),
        )
        asked.append(jnp.concatenate([first.astype(jnp.bfloat16), second.astype(jnp.bfloat16)], axis=1))
    query = jnp.concatenate(asked, axis=0)
    scale = 1.0 / math.sqrt(HEAD)
    dims = (((1,), (1,)), ((), ()))
    old = lax.dot_general(query, past[:, :HEAD], dims, preferred_element_type=jnp.float32) * scale
    new = lax.dot_general(query, keys[...], dims, preferred_element_type=jnp.float32) * scale
    slot = lax.broadcasted_iota(jnp.int32, (1, old.shape[1]), 1)
    old = jnp.where(slot < length, old, -jnp.inf)
    row = lax.broadcasted_iota(jnp.int32, new.shape, 0) % size + starts[-1]
    column = lax.broadcasted_iota(jnp.int32, new.shape, 1)
    new = jnp.where(column <= row, new, -jnp.inf)
    top = jnp.maximum(jnp.max(old, axis=1, keepdims=True), jnp.max(new, axis=1, keepdims=True))
    old = jnp.exp(old - top)
    new = jnp.exp(new - top)
    total = jnp.sum(old, axis=1, keepdims=True) + jnp.sum(new, axis=1, keepdims=True)
    summed = jnp.dot(old.astype(jnp.bfloat16), past[:, HEAD:], preferred_element_type=jnp.float32)
    summed += jnp.dot(new.astype(jnp.bfloat16), values[...], preferred_element_type=jnp.float32)
    result = (summed / total).astype(jnp.bfloat16)
    for h in range(heads):
        out[:, h * HEAD : (h + 1) * HEAD] = result[h * size : (h + 1) * size]


def attend(info, queries, cosine, sine, past, pairs, far=False):
    parts = len(queries)
    size = queries[0].shape[0]
    columns = queries[0].shape[1] - pairs[0][0].shape[1]
    heads = columns // HEAD
    at_once = 2 if heads % 2 == 0 else 1
    operands = [*queries, cosine, sine, past, *[p for group in pairs for p in group]]
    sizes = tuple(group[0].shape[0] for group in pairs)
    fresh = sum(sizes)
    return pl.pallas_call(
        functools.partial(attend_kernel, sizes, at_once, parts),
        grid_spec=pltpu.PrefetchScalarGridSpec(
            num_scalar_prefetch=1,
            grid=(heads // at_once,),
            in_specs=[pl.BlockSpec(memory_space=pl.ANY)] * len(operands),
            out_specs=pl.BlockSpec((size, at_once * HEAD), lambda h, w: (0, h)),
            scratch_shapes=[pltpu.VMEM(a.shape, a.dtype) for a in operands]
            + [
                pltpu.VMEM((fresh, HEAD), jnp.bfloat16),
                pltpu.VMEM((fresh, HEAD), jnp.bfloat16),
                pltpu.SemaphoreType.DMA((len(operands),)),
            ],
        ),
        out_shape=jax.ShapeDtypeStruct((size, columns), jnp.bfloat16),
        compiler_params=pltpu.CompilerParams(vmem_limit_bytes=VMEM),
        cost_estimate=FREE,
    )(info, *(map(in_hbm, queries) if far else queries), *map(in_hbm, operands[parts : parts + 3]), *operands[parts + 3 :])


def solution(mesh):
    n_gx = mesh.shape["gx"]
    n_yz = mesh.shape["yz"]
    inner = n_yz // n_gx
    groups = [[z * inner + r for r in range(inner)] for z in range(n_gx)]
    swap = [(j, j ^ 1) for j in range(n_yz)]

    def tie(value, earlier):
        return lax.optimization_barrier((value, earlier))[0]

    def hop(block, k):
        pairs = [(a * inner + b, (a ^ k) * inner + b) for a in range(n_gx) for b in range(inner)]
        return lax.ppermute(block, "yz", pairs)

    def around(block, end=n_gx):
        return complete([block], end)

    def complete(held, end=n_gx):
        held = list(held)
        for m in range(len(held), end):
            low = m & -m
            block = held[m - low]
            held.append(hop(tie(block, held[1:m]) if m != low else block, low))
        return held

    def turn(picks):
        return [exchange(block, k) for k, block in enumerate(picks)]

    def exchange(block, k):
        if k == 0:
            return block
        return lax.ppermute(block, "gx", [(s, s ^ k) for s in range(n_gx)])

    def times(rows, other, which, weight, extra=None, far=False):
        if inner == 2:
            return product(which, rows, other, weight, extra, far)
        if extra is not None:
            weight = jnp.concatenate([weight, extra], axis=1)
        out = jnp.dot(other, weight, preferred_element_type=jnp.float32)
        out = out.reshape(n_gx, -1, weight.shape[1])
        return [out[0]] + [out[k].astype(jnp.bfloat16) for k in range(1, n_gx)]

    def partner(rows, joined):
        if inner == 2:
            if joined == 1:
                rows = [tie(rows[0], rows[1]), *rows[1:]]
            else:
                rows = [join(rows[i : i + joined]) for i in range(0, n_gx, joined)]
            return [lax.ppermute(block, "yz", swap) for block in rows]
        rows = jnp.concatenate(rows, axis=0)
        return lax.all_gather(rows, "yz", axis=1, tiled=True, axis_index_groups=groups)

    def give(partial):
        return [exchange(p, k) for k, p in enumerate(partial)]

    def collect(partial):
        total = partial[0]
        for p in partial[1:]:
            total = total + p.astype(jnp.float32)
        return total.astype(jnp.bfloat16)

    def pair_columns(part, r):
        if inner == 2:
            other = lax.ppermute(part, "yz", swap)
            return jnp.concatenate(
                [jnp.where(r == 0, part, other), jnp.where(r == 0, other, part)], axis=1
            )
        return lax.all_gather(part, "yz", axis=1, tiled=True, axis_index_groups=groups)

    def across(part):
        return [part] + [hop(part, k) for k in range(1, n_gx)]

    def body(tokens, gain, w_query, w_keyval, w_out, cache, lengths):
        gx = lax.axis_index("gx")
        yz = lax.axis_index("yz")
        z = yz // inner
        r = yz % inner
        _, span, width = tokens.shape
        features = width * n_yz
        pair_columns_here = inner * w_keyval.shape[1]
        ends = [span * sum(SHARES[: t + 1]) // sum(SHARES) for t in range(len(SHARES))]
        parts = [slice(start, end) for start, end in zip([0] + ends, ends)]
        length = lengths[0]

        first = around(tokens[0, parts[0]])

        values = tokens[0].astype(jnp.float32)
        mine = jnp.mean(values, axis=-1)
        moment = jnp.sum(jnp.square(values - mine[:, None]), axis=-1)
        stats = pair_columns(jnp.stack([mine, moment])[:, None], r)
        if inner == 2:
            w_keyval = w_keyval.T
            w_keyval = [w_keyval, lax.ppermute(w_keyval, "yz", swap)]
            stats = tie(stats, w_keyval)
        else:
            w_keyval = pair_columns(w_keyval, r)
        stats = jnp.concatenate(across(stats), axis=1)
        mean = jnp.mean(stats[0], axis=0)
        moments = jnp.sum(stats[1], axis=0) + width * jnp.sum(
            jnp.square(stats[0] - mean), axis=0
        )
        factor = lax.rsqrt(moments / features + 1e-06)
        gains = gain.reshape(n_gx, inner, width)[gx ^ jnp.arange(n_gx), r]
        which = r[None]
        info = jnp.stack([length, z])
        freq = jnp.exp(jnp.arange(HALF, dtype=jnp.float32) * (-2.0 * math.log(10000.0) / HEAD))
        positions = length + jnp.arange(span, dtype=jnp.int32)
        angles = positions.astype(jnp.float32)[:, None] * freq
        cosine = jnp.cos(angles)
        sine = jnp.sin(angles)

        index = z ^ gx ^ jnp.arange(n_gx, dtype=jnp.int32)
        order = [range(1, n_gx - 1), [n_gx - 1, 0]]
        shares = [
            (jnp.stack([z ^ gx ^ k for k in ks]), jnp.stack([gains[k] for k in ks])) for ks in order
        ]
        mean, factor, shares = tie(
            (mean[:, None], factor[:, None], shares), (cosine, sine, info, which, index)
        )

        def normalised(t, held, earlier=()):
            picks = {}
            for ks, (some, scale) in zip(order, shares):
                blocks = normalise(some, mean[parts[t]], factor[parts[t]], scale, held)
                picks.update(zip(ks, blocks))
                held = tie(held, (blocks, earlier))
            return [picks[k] for k in range(n_gx)]

        pairs = []

        def fresh(queries):
            return across(tail_sum(queries, pair_columns_here))

        second = around(tie(tokens[0, parts[1]], first[3]))
        rows = turn(normalised(0, first))
        rows[-1] = tie(rows[-1], second[1:3])
        other = partner(rows, 1)
        partial = times(rows, other, which, w_query, w_keyval, True)
        queries = give(partial)
        pairs.append(fresh(queries))

        picks = normalised(1, tie(second, partial[0]), queries)
        past = lax.all_gather(tie(cache, picks[1]), "yz", axis=1, tiled=True)[0]
        rows = turn(picks)
        heads = attend(info, tie(queries, picks[0]), cosine, sine, past, pairs, True)
        first = around(heads)

        rows = tie(rows, first[1:3])
        other = partner(rows, 2)
        picks = pick(index, first)
        first_rows = turn(picks)
        rows, other = tie((rows, other), picks)
        partial = times(rows, other, which, w_query, w_keyval)
        queries = give(partial)

        rows = tie(first_rows, partial[0])
        partial = times(rows, partner(rows, 4), which, w_out)
        outs = [give(partial)]

        queries = tie(queries, partial[0])
        pairs.append(fresh(queries))
        heads = attend(info, queries, cosine, sine, past, pairs)
        rows = turn(pick(index, tie(around(heads), outs[0][1:3])))
        outs.append(give(times(rows, partner(rows, 4), which, w_out)))
        outs = [collect(o) for o in outs]
        return jnp.concatenate(outs, axis=0)[None]

    return jax.shard_map(
        body,
        mesh=mesh,
        in_specs=(
            P("gx", None, "yz"),
            P(),
            P("gx", "yz"),
            P("gx", "yz"),
            P("gx", "yz"),
            P("gx", "yz", None),
            P("gx"),
        ),
        out_specs=P("gx", None, "yz"),
        check_vma=False,
    )
```

```python
import functools
import math

import jax
import jax.numpy as jnp
from jax import lax
from jax.experimental import pallas as pl
from jax.experimental.pallas import tpu as pltpu
from jax.sharding import PartitionSpec as P

HEAD = 256
HALF = HEAD // 2
SHARES = (4, 4)
VMEM = 26 << 20
STRIPS = 4
FREE = pl.CostEstimate(flops=0, bytes_accessed=0, transcendentals=0)


def in_hbm(array):
    return pltpu.with_memory_space_constraint(array, pltpu.HBM)


def pick_kernel(parts, index, *refs):
    held, outs, sems = refs[:parts], refs[parts:-1], refs[-1]
    for k, out in enumerate(outs):
        for m, block in enumerate(held):

            @pl.when(index[k] == m)
            def _():
                pltpu.make_async_copy(block, out, sems.at[k]).start()

    for k, out in enumerate(outs):
        pltpu.make_async_copy(held[0], out, sems.at[k]).wait()


def pick(index, held):
    parts = len(held)
    block = held[0]
    return pl.pallas_call(
        functools.partial(pick_kernel, parts),
        grid_spec=pltpu.PrefetchScalarGridSpec(
            num_scalar_prefetch=1,
            grid=(),
            in_specs=[pl.BlockSpec(memory_space=pl.ANY)] * parts,
            out_specs=[pl.BlockSpec(memory_space=pl.ANY)] * parts,
            scratch_shapes=[pltpu.SemaphoreType.DMA((parts,))],
        ),
        out_shape=[jax.ShapeDtypeStruct(block.shape, block.dtype)] * parts,
        compiler_params=pltpu.CompilerParams(vmem_limit_bytes=VMEM),
        cost_estimate=FREE,
    )(index, *held)


def normalise_kernel(parts, index, mean, factor, gains, *refs):
    outs, held, blocks, sems = refs[-2 - parts : -2], refs[: -2 - parts], refs[-2], refs[-1]
    for k in range(parts):
        for m, block in enumerate(held):

            @pl.when(index[k] == m)
            def _():
                pltpu.make_async_copy(block, blocks.at[k], sems.at[k]).start()

    for k, out in enumerate(outs):
        pltpu.make_async_copy(held[0], blocks.at[k], sems.at[k]).wait()
        gain = gains[k : k + 1, :]

        @pl.loop(0, out.shape[0], step=32)
        def _(start):
            rows = pl.ds(pl.multiple_of(start, 32), 32)
            centred = blocks[k, rows, :].astype(jnp.float32) - mean[rows, :]
            out[rows, :] = (centred * factor[rows, :] * gain).astype(out.dtype)


def normalise(index, mean, factor, gains, held):
    parts = index.shape[0]
    block = held[0]
    inside = pl.BlockSpec(memory_space=pltpu.VMEM)
    return pl.pallas_call(
        functools.partial(normalise_kernel, parts),
        grid_spec=pltpu.PrefetchScalarGridSpec(
            num_scalar_prefetch=1,
            grid=(),
            in_specs=[inside] * 3 + [pl.BlockSpec(memory_space=pl.ANY)] * len(held),
            out_specs=[inside] * parts,
            scratch_shapes=[
                pltpu.VMEM((parts, *block.shape), block.dtype),
                pltpu.SemaphoreType.DMA((parts,)),
            ],
        ),
        out_shape=[jax.ShapeDtypeStruct(block.shape, block.dtype)] * parts,
        compiler_params=pltpu.CompilerParams(vmem_limit_bytes=VMEM),
        cost_estimate=FREE,
    )(index, mean, factor, gains, *held)


def join_kernel(*refs):
    *pieces, out, sems = refs
    size = pieces[0].shape[0]
    copies = [
        pltpu.make_async_copy(piece, out.at[pl.ds(i * size, size)], sems.at[i])
        for i, piece in enumerate(pieces)
    ]
    for copy in copies:
        copy.start()
    for copy in copies:
        copy.wait()


def join(pieces):
    size, columns = pieces[0].shape
    return pl.pallas_call(
        join_kernel,
        in_specs=[pl.BlockSpec(memory_space=pl.ANY)] * len(pieces),
        out_specs=pl.BlockSpec(memory_space=pl.ANY),
        scratch_shapes=[pltpu.SemaphoreType.DMA((len(pieces),))],
        out_shape=jax.ShapeDtypeStruct((len(pieces) * size, columns), pieces[0].dtype),
        compiler_params=pltpu.CompilerParams(vmem_limit_bytes=VMEM),
        cost_estimate=FREE,
    )(*pieces)


def tail_kernel(*refs):
    *parts, out = refs
    total = parts[0][...]
    for part in parts[1:]:
        total += part[...].astype(jnp.float32)
    out[...] = total.astype(out.dtype)


def tail_sum(parts, columns):
    size, total = parts[0].shape
    last = total // columns - 1
    return pl.pallas_call(
        tail_kernel,
        grid=(1,),
        in_specs=[pl.BlockSpec((size, columns), lambda i: (0, last))] * len(parts),
        out_specs=pl.BlockSpec((size, columns), lambda i: (0, 0)),
        out_shape=jax.ShapeDtypeStruct((size, columns), jnp.bfloat16),
        compiler_params=pltpu.CompilerParams(vmem_limit_bytes=VMEM),
        cost_estimate=FREE,
    )(*parts)


def widest(columns):
    for width in (768, 512, 256):
        if columns % width == 0:
            return width
    return columns


def product_kernel(groups, joined, which, *refs):
    near_pieces, far_pieces, refs = refs[:groups], refs[groups : groups + joined], refs[groups + joined :]
    weight, refs = refs[0], refs[1:]
    extra, narrow = None, None
    if len(refs) > groups + 4:
        extra, narrow, refs = refs[:2], refs[-1], refs[2:-1]
    outs, (rows, tiles, sums, sems) = refs[:groups], refs[groups:]
    blocks, _, deep = rows.shape
    size, depth = near_pieces[0].shape
    columns = weight.shape[1]
    shares = blocks // 2
    width = widest(columns)

    waits = []
    for block in range(blocks):
        half, share = block // shares, block % shares
        mine = half == 0
        row = pl.multiple_of((which[0] if mine else 1 - which[0]) * depth + share * deep, deep)
        part = slice(share * deep, (share + 1) * deep)
        pieces = near_pieces if mine else far_pieces
        tall = groups * size // len(pieces)
        moves = [
            (piece.at[:, part], rows.at[block, pl.ds(i * tall, tall)]) for i, piece in enumerate(pieces)
        ]
        strip = deep // STRIPS
        for i in range(STRIPS):
            moves.append(
                (
                    weight.at[pl.ds(pl.multiple_of(row + i * strip, strip), strip)],
                    tiles.at[block, pl.ds(i * strip, strip)],
                )
            )
        if extra is not None:
            for other, source in enumerate(extra):
                high = source.shape[0]
                place = which[0] if other == 0 else 1 - which[0]
                moves.append(
                    (
                        source.at[:, pl.ds(row, deep)],
                        narrow.at[block, pl.ds(pl.multiple_of(place * high, high), high)],
                    )
                )
        waits.append(
            [pltpu.make_async_copy(a, b, sems.at[block, i]) for i, (a, b) in enumerate(moves)]
        )
    for copy in waits[0] + waits[1]:
        copy.start()

    def add(total, place, block):
        if block:
            total += sums[:, place]
        if block < blocks - 1:
            sums[:, place] = total
        else:
            for k, out in enumerate(outs):
                out[:, place] = total[k * size : (k + 1) * size].astype(out.dtype)

    for block, copies in enumerate(waits):
        for copy in copies:
            copy.wait()
        if block + 2 < blocks:
            for copy in waits[block + 2]:
                copy.start()
        if extra is not None:
            total = lax.dot_general(
                rows[block], narrow[block], (((1,), (1,)), ((), ())), preferred_element_type=jnp.float32
            )
            add(total, slice(columns, None), block)

        @pl.loop(0, columns // width)
        def _(j):
            place = pl.ds(pl.multiple_of(j * width, width), width)
            total = jnp.dot(rows[block], tiles[block, :, place], preferred_element_type=jnp.float32)
            add(total, place, block)


def product(which, own, other, weight, extra=None, far=False):
    groups = len(own)
    size, depth = own[0].shape
    columns = weight.shape[1]
    shares = 2 if depth % 256 == 0 and depth > 1024 else 1
    deep = depth // shares
    weights = [weight]
    total = columns
    if extra is not None:
        weights += extra
        total += 2 * extra[0].shape[0]
    scratch = [
        pltpu.VMEM((2 * shares, groups * size, deep), jnp.bfloat16),
        pltpu.VMEM((2 * shares, deep, columns), jnp.bfloat16),
        pltpu.VMEM((groups * size, total), jnp.float32),
        pltpu.SemaphoreType.DMA((2 * shares, groups + STRIPS + 2)),
    ]
    if extra is not None:
        scratch.append(pltpu.VMEM((2 * shares, total - columns, deep), jnp.bfloat16))
    if far:
        own = map(in_hbm, own)
    operands = [*own, *other, *map(in_hbm, weights)]
    return pl.pallas_call(
        functools.partial(product_kernel, groups, len(other)),
        grid_spec=pltpu.PrefetchScalarGridSpec(
            num_scalar_prefetch=1,
            grid=(),
            in_specs=[pl.BlockSpec(memory_space=pl.ANY)] * len(operands),
            out_specs=[pl.BlockSpec(memory_space=pltpu.VMEM)] * groups,
            scratch_shapes=scratch,
        ),
        out_shape=[
            jax.ShapeDtypeStruct((size, total), jnp.bfloat16 if k else jnp.float32) for k in range(groups)
        ],
        compiler_params=pltpu.CompilerParams(vmem_limit_bytes=VMEM),
        cost_estimate=FREE
        if extra is not None
        else pl.CostEstimate(flops=8 * groups * size * depth * total, bytes_accessed=0, transcendentals=0),
    )(which, *operands)


def attend_kernel(sizes, heads, parts, info, *refs):
    chunk = len(sizes) - 1
    size = sizes[-1]
    starts = [sum(sizes[:c]) for c in range(len(sizes))]
    count = parts + 3 + parts * (chunk + 1)
    sources, out, held = refs[:count], refs[count], refs[count + 1 : -3]
    keys, values, sems = refs[-3:]
    queries, held = held[:parts], held[parts:]
    cosine, sine, past = held[:3]
    pairs = held[3:]
    length = info[0]
    z = info[1]
    step = pl.program_id(0)

    def turned(first, second, rows):
        cos = cosine[rows, :]
        sin = sine[rows, :]
        return first * cos - second * sin, second * cos + first * sin

    @pl.when(step == 0)
    def _():
        copies = [
            pltpu.make_async_copy(source, target, sems.at[i])
            for i, (source, target) in enumerate(zip(sources, refs[count + 1 : -3]))
        ]
        for copy in copies:
            copy.start()
        for copy in copies:
            copy.wait()
        for c in range(chunk + 1):
            rows = slice(starts[c], starts[c] + sizes[c])
            found = []
            for a in range(parts):
                block = pairs[c * parts][...]
                for k in range(1, parts):
                    block = jnp.where(z == a ^ k, pairs[c * parts + k][...], block)
                found.append(block)
            joined = jnp.concatenate(found, axis=1)
            first, second = turned(
                joined[:, :HALF].astype(jnp.float32), joined[:, HALF:HEAD].astype(jnp.float32), rows
            )
            keys[rows, :HALF] = first.astype(jnp.bfloat16)
            keys[rows, HALF:] = second.astype(jnp.bfloat16)
            values[rows, :] = joined[:, HEAD:]

    here = pl.ds(pl.multiple_of(step * (heads * HEAD), heads * HEAD), heads * HEAD)
    raw = queries[0][:, here]
    for k in range(1, parts):
        raw = raw + queries[k][:, here].astype(jnp.float32)
    asked = []
    for h in range(heads):
        first, second = turned(
            raw[:, h * HEAD : h * HEAD + HALF],
            raw[:, h * HEAD + HALF : (h + 1) * HEAD],
            slice(starts[-1], starts[-1] + size),
        )
        asked.append(jnp.concatenate([first.astype(jnp.bfloat16), second.astype(jnp.bfloat16)], axis=1))
    query = jnp.concatenate(asked, axis=0)
    scale = 1.0 / math.sqrt(HEAD)
    dims = (((1,), (1,)), ((), ()))
    old = lax.dot_general(query, past[:, :HEAD], dims, preferred_element_type=jnp.float32) * scale
    new = lax.dot_general(query, keys[...], dims, preferred_element_type=jnp.float32) * scale
    slot = lax.broadcasted_iota(jnp.int32, (1, old.shape[1]), 1)
    old = jnp.where(slot < length, old, -jnp.inf)
    row = lax.broadcasted_iota(jnp.int32, new.shape, 0) % size + starts[-1]
    column = lax.broadcasted_iota(jnp.int32, new.shape, 1)
    new = jnp.where(column <= row, new, -jnp.inf)
    top = jnp.maximum(jnp.max(old, axis=1, keepdims=True), jnp.max(new, axis=1, keepdims=True))
    old = jnp.exp(old - top)
    new = jnp.exp(new - top)
    total = jnp.sum(old, axis=1, keepdims=True) + jnp.sum(new, axis=1, keepdims=True)
    summed = jnp.dot(old.astype(jnp.bfloat16), past[:, HEAD:], preferred_element_type=jnp.float32)
    summed += jnp.dot(new.astype(jnp.bfloat16), values[...], preferred_element_type=jnp.float32)
    result = (summed / total).astype(jnp.bfloat16)
    for h in range(heads):
        out[:, h * HEAD : (h + 1) * HEAD] = result[h * size : (h + 1) * size]


def attend(info, queries, cosine, sine, past, pairs, far=False):
    parts = len(queries)
    size = queries[0].shape[0]
    columns = queries[0].shape[1] - pairs[0][0].shape[1]
    heads = columns // HEAD
    at_once = 2 if heads % 2 == 0 else 1
    operands = [*queries, cosine, sine, past, *[p for group in pairs for p in group]]
    sizes = tuple(group[0].shape[0] for group in pairs)
    fresh = sum(sizes)
    return pl.pallas_call(
        functools.partial(attend_kernel, sizes, at_once, parts),
        grid_spec=pltpu.PrefetchScalarGridSpec(
            num_scalar_prefetch=1,
            grid=(heads // at_once,),
            in_specs=[pl.BlockSpec(memory_space=pl.ANY)] * len(operands),
            out_specs=pl.BlockSpec((size, at_once * HEAD), lambda h, w: (0, h)),
            scratch_shapes=[pltpu.VMEM(a.shape, a.dtype) for a in operands]
            + [
                pltpu.VMEM((fresh, HEAD), jnp.bfloat16),
                pltpu.VMEM((fresh, HEAD), jnp.bfloat16),
                pltpu.SemaphoreType.DMA((len(operands),)),
            ],
        ),
        out_shape=jax.ShapeDtypeStruct((size, columns), jnp.bfloat16),
        compiler_params=pltpu.CompilerParams(vmem_limit_bytes=VMEM),
        cost_estimate=pl.CostEstimate(
            flops=16 * size * columns * (past.shape[0] + fresh), bytes_accessed=0, transcendentals=0
        ),
    )(info, *(map(in_hbm, queries) if far else queries), *map(in_hbm, operands[parts : parts + 3]), *operands[parts + 3 :])


def solution(mesh):
    n_gx = mesh.shape["gx"]
    n_yz = mesh.shape["yz"]
    inner = n_yz // n_gx
    groups = [[z * inner + r for r in range(inner)] for z in range(n_gx)]
    swap = [(j, j ^ 1) for j in range(n_yz)]

    def tie(value, earlier):
        return lax.optimization_barrier((value, earlier))[0]

    def hop(block, k):
        pairs = [(a * inner + b, (a ^ k) * inner + b) for a in range(n_gx) for b in range(inner)]
        return lax.ppermute(block, "yz", pairs)

    def around(block, end=n_gx):
        return complete([block], end)

    def complete(held, end=n_gx):
        held = list(held)
        for m in range(len(held), end):
            low = m & -m
            block = held[m - low]
            held.append(hop(tie(block, held[1:m]) if m != low else block, low))
        return held

    def turn(picks):
        return [exchange(block, k) for k, block in enumerate(picks)]

    def exchange(block, k):
        if k == 0:
            return block
        return lax.ppermute(block, "gx", [(s, s ^ k) for s in range(n_gx)])

    def times(rows, other, which, weight, extra=None, far=False):
        if inner == 2:
            return product(which, rows, other, weight, extra, far)
        if extra is not None:
            weight = jnp.concatenate([weight, extra], axis=1)
        out = jnp.dot(other, weight, preferred_element_type=jnp.float32)
        out = out.reshape(n_gx, -1, weight.shape[1])
        return [out[0]] + [out[k].astype(jnp.bfloat16) for k in range(1, n_gx)]

    def partner(rows, joined):
        if inner == 2:
            if joined == 1:
                rows = [tie(rows[0], rows[1]), *rows[1:]]
            else:
                rows = [join(rows[i : i + joined]) for i in range(0, n_gx, joined)]
            return [lax.ppermute(block, "yz", swap) for block in rows]
        rows = jnp.concatenate(rows, axis=0)
        return lax.all_gather(rows, "yz", axis=1, tiled=True, axis_index_groups=groups)

    def give(partial):
        return [exchange(p, k) for k, p in enumerate(partial)]

    def collect(partial):
        total = partial[0]
        for p in partial[1:]:
            total = total + p.astype(jnp.float32)
        return total.astype(jnp.bfloat16)

    def pair_columns(part, r):
        if inner == 2:
            other = lax.ppermute(part, "yz", swap)
            return jnp.concatenate(
                [jnp.where(r == 0, part, other), jnp.where(r == 0, other, part)], axis=1
            )
        return lax.all_gather(part, "yz", axis=1, tiled=True, axis_index_groups=groups)

    def across(part):
        return [part] + [hop(part, k) for k in range(1, n_gx)]

    def body(tokens, gain, w_query, w_keyval, w_out, cache, lengths):
        gx = lax.axis_index("gx")
        yz = lax.axis_index("yz")
        z = yz // inner
        r = yz % inner
        _, span, width = tokens.shape
        features = width * n_yz
        pair_columns_here = inner * w_keyval.shape[1]
        ends = [span * sum(SHARES[: t + 1]) // sum(SHARES) for t in range(len(SHARES))]
        parts = [slice(start, end) for start, end in zip([0] + ends, ends)]
        length = lengths[0]

        first = around(tokens[0, parts[0]])

        values = tokens[0].astype(jnp.float32)
        mine = jnp.mean(values, axis=-1)
        moment = jnp.sum(jnp.square(values - mine[:, None]), axis=-1)
        stats = pair_columns(jnp.stack([mine, moment])[:, None], r)
        if inner == 2:
            w_keyval = w_keyval.T
            w_keyval = [w_keyval, lax.ppermute(w_keyval, "yz", swap)]
            stats = tie(stats, w_keyval)
        else:
            w_keyval = pair_columns(w_keyval, r)
        stats = jnp.concatenate(across(stats), axis=1)
        mean = jnp.mean(stats[0], axis=0)
        moments = jnp.sum(stats[1], axis=0) + width * jnp.sum(
            jnp.square(stats[0] - mean), axis=0
        )
        factor = lax.rsqrt(moments / features + 1e-06)
        gains = gain.reshape(n_gx, inner, width)[gx ^ jnp.arange(n_gx), r]
        which = r[None]
        info = jnp.stack([length, z])
        freq = jnp.exp(jnp.arange(HALF, dtype=jnp.float32) * (-2.0 * math.log(10000.0) / HEAD))
        positions = length + jnp.arange(span, dtype=jnp.int32)
        angles = positions.astype(jnp.float32)[:, None] * freq
        cosine = jnp.cos(angles)
        sine = jnp.sin(angles)

        index = z ^ gx ^ jnp.arange(n_gx, dtype=jnp.int32)
        order = [range(1, n_gx - 1), [n_gx - 1, 0]]
        shares = [
            (jnp.stack([z ^ gx ^ k for k in ks]), jnp.stack([gains[k] for k in ks])) for ks in order
        ]
        mean, factor, shares = tie(
            (mean[:, None], factor[:, None], shares), (cosine, sine, info, which, index)
        )

        def normalised(t, held, earlier=()):
            picks = {}
            for ks, (some, scale) in zip(order, shares):
                blocks = normalise(some, mean[parts[t]], factor[parts[t]], scale, held)
                picks.update(zip(ks, blocks))
                held = tie(held, (blocks, earlier))
            return [picks[k] for k in range(n_gx)]

        pairs = []

        def fresh(queries):
            return across(tail_sum(queries, pair_columns_here))

        picks = normalised(0, first)
        second = around(tie(tokens[0, parts[1]], picks[0]))
        rows = turn(picks)
        rows[-1] = tie(rows[-1], second[1:3])
        other = partner(rows, 1)
        partial = times(rows, other, which, w_query, w_keyval, True)
        queries = give(partial)
        pairs.append(fresh(queries))

        picks = normalised(1, tie(second, partial[0]), queries)
        past = lax.all_gather(tie(cache, picks[1]), "yz", axis=1, tiled=True)[0]
        rows = turn(picks)
        heads = attend(info, tie(queries, picks[0]), cosine, sine, past, pairs, True)
        first = around(heads)
        rows = tie(rows, heads)
        partial = times(rows, partner(rows, 2), which, w_query, w_keyval)
        queries = give(partial)
        pairs.append(fresh(queries))
        rows = turn(pick(index, tie(first, (queries[1:], pairs[1][1]))))
        heads = attend(info, queries, cosine, sine, past, pairs)
        second = around(heads, 3)

        partial = times(tie(rows, heads), partner(tie(rows, heads), 4), which, w_out)
        outs = [give(partial)]
        rows = turn(pick(index, complete(tie(second, partial[0]))))
        outs.append(give(times(rows, partner(tie(rows, outs[0][1:3]), 4), which, w_out)))
        outs = [collect(o) for o in outs]
        return jnp.concatenate(outs, axis=0)[None]

    return jax.shard_map(
        body,
        mesh=mesh,
        in_specs=(
            P("gx", None, "yz"),
            P(),
            P("gx", "yz"),
            P("gx", "yz"),
            P("gx", "yz"),
            P("gx", "yz", None),
            P("gx"),
        ),
        out_specs=P("gx", None, "yz"),
        check_vma=False,
    )
```

```python
import functools
import math

import jax
import jax.numpy as jnp
from jax import lax
from jax.experimental import pallas as pl
from jax.experimental.pallas import tpu as pltpu
from jax.sharding import PartitionSpec as P

HEAD = 256
HALF = HEAD // 2
SHARES = (4, 4)
VMEM = 26 << 20
STRIPS = 4
FREE = pl.CostEstimate(flops=0, bytes_accessed=0, transcendentals=0)


def in_hbm(array):
    return pltpu.with_memory_space_constraint(array, pltpu.HBM)


def pick_kernel(parts, index, *refs):
    held, outs, sems = refs[:parts], refs[parts:-1], refs[-1]
    for k, out in enumerate(outs):
        for m, block in enumerate(held):

            @pl.when(index[k] == m)
            def _():
                pltpu.make_async_copy(block, out, sems.at[k]).start()

    for k, out in enumerate(outs):
        pltpu.make_async_copy(held[0], out, sems.at[k]).wait()


def pick(index, held):
    parts = len(held)
    block = held[0]
    return pl.pallas_call(
        functools.partial(pick_kernel, parts),
        grid_spec=pltpu.PrefetchScalarGridSpec(
            num_scalar_prefetch=1,
            grid=(),
            in_specs=[pl.BlockSpec(memory_space=pl.ANY)] * parts,
            out_specs=[pl.BlockSpec(memory_space=pl.ANY)] * parts,
            scratch_shapes=[pltpu.SemaphoreType.DMA((parts,))],
        ),
        out_shape=[jax.ShapeDtypeStruct(block.shape, block.dtype)] * parts,
        compiler_params=pltpu.CompilerParams(vmem_limit_bytes=VMEM),
        cost_estimate=FREE,
    )(index, *held)


def normalise_kernel(parts, index, mean, factor, gains, *refs):
    outs, held, blocks, sems = refs[-2 - parts : -2], refs[: -2 - parts], refs[-2], refs[-1]
    for k in range(parts):
        for m, block in enumerate(held):

            @pl.when(index[k] == m)
            def _():
                pltpu.make_async_copy(block, blocks.at[k], sems.at[k]).start()

    for k, out in enumerate(outs):
        pltpu.make_async_copy(held[0], blocks.at[k], sems.at[k]).wait()
        gain = gains[k : k + 1, :]

        @pl.loop(0, out.shape[0], step=32)
        def _(start):
            rows = pl.ds(pl.multiple_of(start, 32), 32)
            centred = blocks[k, rows, :].astype(jnp.float32) - mean[rows, :]
            out[rows, :] = (centred * factor[rows, :] * gain).astype(out.dtype)


def normalise(index, mean, factor, gains, held):
    parts = index.shape[0]
    block = held[0]
    inside = pl.BlockSpec(memory_space=pltpu.VMEM)
    return pl.pallas_call(
        functools.partial(normalise_kernel, parts),
        grid_spec=pltpu.PrefetchScalarGridSpec(
            num_scalar_prefetch=1,
            grid=(),
            in_specs=[inside] * 3 + [pl.BlockSpec(memory_space=pl.ANY)] * len(held),
            out_specs=[inside] * parts,
            scratch_shapes=[
                pltpu.VMEM((parts, *block.shape), block.dtype),
                pltpu.SemaphoreType.DMA((parts,)),
            ],
        ),
        out_shape=[jax.ShapeDtypeStruct(block.shape, block.dtype)] * parts,
        compiler_params=pltpu.CompilerParams(vmem_limit_bytes=VMEM),
        cost_estimate=FREE,
    )(index, mean, factor, gains, *held)


def join_kernel(*refs):
    *pieces, out, sems = refs
    size = pieces[0].shape[0]
    copies = [
        pltpu.make_async_copy(piece, out.at[pl.ds(i * size, size)], sems.at[i])
        for i, piece in enumerate(pieces)
    ]
    for copy in copies:
        copy.start()
    for copy in copies:
        copy.wait()


def join(pieces):
    size, columns = pieces[0].shape
    return pl.pallas_call(
        join_kernel,
        in_specs=[pl.BlockSpec(memory_space=pl.ANY)] * len(pieces),
        out_specs=pl.BlockSpec(memory_space=pl.ANY),
        scratch_shapes=[pltpu.SemaphoreType.DMA((len(pieces),))],
        out_shape=jax.ShapeDtypeStruct((len(pieces) * size, columns), pieces[0].dtype),
        compiler_params=pltpu.CompilerParams(vmem_limit_bytes=VMEM),
        cost_estimate=FREE,
    )(*pieces)


def tail_kernel(*refs):
    *parts, out = refs
    total = parts[0][...]
    for part in parts[1:]:
        total += part[...].astype(jnp.float32)
    out[...] = total.astype(out.dtype)


def tail_sum(parts, columns):
    size, total = parts[0].shape
    last = total // columns - 1
    return pl.pallas_call(
        tail_kernel,
        grid=(1,),
        in_specs=[pl.BlockSpec((size, columns), lambda i: (0, last))] * len(parts),
        out_specs=pl.BlockSpec((size, columns), lambda i: (0, 0)),
        out_shape=jax.ShapeDtypeStruct((size, columns), jnp.bfloat16),
        compiler_params=pltpu.CompilerParams(vmem_limit_bytes=VMEM),
        cost_estimate=FREE,
    )(*parts)


def widest(columns):
    for width in (768, 512, 256):
        if columns % width == 0:
            return width
    return columns


def product_kernel(groups, joined, which, *refs):
    near_pieces, far_pieces, refs = refs[:groups], refs[groups : groups + joined], refs[groups + joined :]
    weight, refs = refs[0], refs[1:]
    extra, narrow = None, None
    if len(refs) > groups + 4:
        extra, narrow, refs = refs[:2], refs[-1], refs[2:-1]
    outs, (rows, tiles, sums, sems) = refs[:groups], refs[groups:]
    blocks, _, deep = rows.shape
    size, depth = near_pieces[0].shape
    columns = weight.shape[1]
    shares = blocks // 2
    width = widest(columns)

    waits = []
    for block in range(blocks):
        half, share = block // shares, block % shares
        mine = half == 0
        row = pl.multiple_of((which[0] if mine else 1 - which[0]) * depth + share * deep, deep)
        part = slice(share * deep, (share + 1) * deep)
        pieces = near_pieces if mine else far_pieces
        tall = groups * size // len(pieces)
        moves = [
            (piece.at[:, part], rows.at[block, pl.ds(i * tall, tall)]) for i, piece in enumerate(pieces)
        ]
        strip = deep // STRIPS
        for i in range(STRIPS):
            moves.append(
                (
                    weight.at[pl.ds(pl.multiple_of(row + i * strip, strip), strip)],
                    tiles.at[block, pl.ds(i * strip, strip)],
                )
            )
        if extra is not None:
            for other, source in enumerate(extra):
                high = source.shape[0]
                place = which[0] if other == 0 else 1 - which[0]
                moves.append(
                    (
                        source.at[:, pl.ds(row, deep)],
                        narrow.at[block, pl.ds(pl.multiple_of(place * high, high), high)],
                    )
                )
        waits.append(
            [pltpu.make_async_copy(a, b, sems.at[block, i]) for i, (a, b) in enumerate(moves)]
        )
    for copy in waits[0] + waits[1]:
        copy.start()

    def add(total, place, block):
        if block:
            total += sums[:, place]
        if block < blocks - 1:
            sums[:, place] = total
        else:
            for k, out in enumerate(outs):
                out[:, place] = total[k * size : (k + 1) * size].astype(out.dtype)

    for block, copies in enumerate(waits):
        for copy in copies:
            copy.wait()
        if block + 2 < blocks:
            for copy in waits[block + 2]:
                copy.start()
        if extra is not None:
            total = lax.dot_general(
                rows[block], narrow[block], (((1,), (1,)), ((), ())), preferred_element_type=jnp.float32
            )
            add(total, slice(columns, None), block)

        @pl.loop(0, columns // width)
        def _(j):
            place = pl.ds(pl.multiple_of(j * width, width), width)
            total = jnp.dot(rows[block], tiles[block, :, place], preferred_element_type=jnp.float32)
            add(total, place, block)


def product(which, own, other, weight, extra=None, far=False):
    groups = len(own)
    size, depth = own[0].shape
    columns = weight.shape[1]
    shares = 2 if depth % 256 == 0 and depth > 1024 else 1
    deep = depth // shares
    weights = [weight]
    total = columns
    if extra is not None:
        weights += extra
        total += 2 * extra[0].shape[0]
    scratch = [
        pltpu.VMEM((2 * shares, groups * size, deep), jnp.bfloat16),
        pltpu.VMEM((2 * shares, deep, columns), jnp.bfloat16),
        pltpu.VMEM((groups * size, total), jnp.float32),
        pltpu.SemaphoreType.DMA((2 * shares, groups + STRIPS + 2)),
    ]
    if extra is not None:
        scratch.append(pltpu.VMEM((2 * shares, total - columns, deep), jnp.bfloat16))
    if far:
        own = map(in_hbm, own)
    operands = [*own, *other, *map(in_hbm, weights)]
    return pl.pallas_call(
        functools.partial(product_kernel, groups, len(other)),
        grid_spec=pltpu.PrefetchScalarGridSpec(
            num_scalar_prefetch=1,
            grid=(),
            in_specs=[pl.BlockSpec(memory_space=pl.ANY)] * len(operands),
            out_specs=[pl.BlockSpec(memory_space=pltpu.VMEM)] * groups,
            scratch_shapes=scratch,
        ),
        out_shape=[
            jax.ShapeDtypeStruct((size, total), jnp.bfloat16 if k else jnp.float32) for k in range(groups)
        ],
        compiler_params=pltpu.CompilerParams(vmem_limit_bytes=VMEM),
        cost_estimate=FREE
        if extra is not None
        else pl.CostEstimate(flops=8 * groups * size * depth * total, bytes_accessed=0, transcendentals=0),
    )(which, *operands)


def attend_kernel(sizes, heads, parts, info, *refs):
    chunk = len(sizes) - 1
    size = sizes[-1]
    starts = [sum(sizes[:c]) for c in range(len(sizes))]
    count = parts + 3 + parts * (chunk + 1)
    sources, out, held = refs[:count], refs[count], refs[count + 1 : -3]
    keys, values, sems = refs[-3:]
    queries, held = held[:parts], held[parts:]
    cosine, sine, past = held[:3]
    pairs = held[3:]
    length = info[0]
    z = info[1]
    step = pl.program_id(0)

    def turned(first, second, rows):
        cos = cosine[rows, :]
        sin = sine[rows, :]
        return first * cos - second * sin, second * cos + first * sin

    @pl.when(step == 0)
    def _():
        copies = [
            pltpu.make_async_copy(source, target, sems.at[i])
            for i, (source, target) in enumerate(zip(sources, refs[count + 1 : -3]))
        ]
        for copy in copies:
            copy.start()
        for copy in copies:
            copy.wait()
        for c in range(chunk + 1):
            rows = slice(starts[c], starts[c] + sizes[c])
            found = []
            for a in range(parts):
                block = pairs[c * parts][...]
                for k in range(1, parts):
                    block = jnp.where(z == a ^ k, pairs[c * parts + k][...], block)
                found.append(block)
            joined = jnp.concatenate(found, axis=1)
            first, second = turned(
                joined[:, :HALF].astype(jnp.float32), joined[:, HALF:HEAD].astype(jnp.float32), rows
            )
            keys[rows, :HALF] = first.astype(jnp.bfloat16)
            keys[rows, HALF:] = second.astype(jnp.bfloat16)
            values[rows, :] = joined[:, HEAD:]

    here = pl.ds(pl.multiple_of(step * (heads * HEAD), heads * HEAD), heads * HEAD)
    raw = queries[0][:, here]
    for k in range(1, parts):
        raw = raw + queries[k][:, here].astype(jnp.float32)
    asked = []
    for h in range(heads):
        first, second = turned(
            raw[:, h * HEAD : h * HEAD + HALF],
            raw[:, h * HEAD + HALF : (h + 1) * HEAD],
            slice(starts[-1], starts[-1] + size),
        )
        asked.append(jnp.concatenate([first.astype(jnp.bfloat16), second.astype(jnp.bfloat16)], axis=1))
    query = jnp.concatenate(asked, axis=0)
    scale = 1.0 / math.sqrt(HEAD)
    dims = (((1,), (1,)), ((), ()))
    old = lax.dot_general(query, past[:, :HEAD], dims, preferred_element_type=jnp.float32) * scale
    new = lax.dot_general(query, keys[...], dims, preferred_element_type=jnp.float32) * scale
    slot = lax.broadcasted_iota(jnp.int32, (1, old.shape[1]), 1)
    old = jnp.where(slot < length, old, -jnp.inf)
    row = lax.broadcasted_iota(jnp.int32, new.shape, 0) % size + starts[-1]
    column = lax.broadcasted_iota(jnp.int32, new.shape, 1)
    new = jnp.where(column <= row, new, -jnp.inf)
    top = jnp.maximum(jnp.max(old, axis=1, keepdims=True), jnp.max(new, axis=1, keepdims=True))
    old = jnp.exp(old - top)
    new = jnp.exp(new - top)
    total = jnp.sum(old, axis=1, keepdims=True) + jnp.sum(new, axis=1, keepdims=True)
    summed = jnp.dot(old.astype(jnp.bfloat16), past[:, HEAD:], preferred_element_type=jnp.float32)
    summed += jnp.dot(new.astype(jnp.bfloat16), values[...], preferred_element_type=jnp.float32)
    result = (summed / total).astype(jnp.bfloat16)
    for h in range(heads):
        out[:, h * HEAD : (h + 1) * HEAD] = result[h * size : (h + 1) * size]


def attend(info, queries, cosine, sine, past, pairs, far=False):
    parts = len(queries)
    size = queries[0].shape[0]
    columns = queries[0].shape[1] - pairs[0][0].shape[1]
    heads = columns // HEAD
    at_once = 2 if heads % 2 == 0 else 1
    operands = [*queries, cosine, sine, past, *[p for group in pairs for p in group]]
    sizes = tuple(group[0].shape[0] for group in pairs)
    fresh = sum(sizes)
    return pl.pallas_call(
        functools.partial(attend_kernel, sizes, at_once, parts),
        grid_spec=pltpu.PrefetchScalarGridSpec(
            num_scalar_prefetch=1,
            grid=(heads // at_once,),
            in_specs=[pl.BlockSpec(memory_space=pl.ANY)] * len(operands),
            out_specs=pl.BlockSpec((size, at_once * HEAD), lambda h, w: (0, h)),
            scratch_shapes=[pltpu.VMEM(a.shape, a.dtype) for a in operands]
            + [
                pltpu.VMEM((fresh, HEAD), jnp.bfloat16),
                pltpu.VMEM((fresh, HEAD), jnp.bfloat16),
                pltpu.SemaphoreType.DMA((len(operands),)),
            ],
        ),
        out_shape=jax.ShapeDtypeStruct((size, columns), jnp.bfloat16),
        compiler_params=pltpu.CompilerParams(vmem_limit_bytes=VMEM),
        cost_estimate=pl.CostEstimate(
            flops=16 * size * columns * (past.shape[0] + fresh), bytes_accessed=0, transcendentals=0
        ),
    )(info, *(map(in_hbm, queries) if far else queries), *map(in_hbm, operands[parts : parts + 3]), *operands[parts + 3 :])


def solution(mesh):
    n_gx = mesh.shape["gx"]
    n_yz = mesh.shape["yz"]
    inner = n_yz // n_gx
    groups = [[z * inner + r for r in range(inner)] for z in range(n_gx)]
    swap = [(j, j ^ 1) for j in range(n_yz)]

    def tie(value, earlier):
        return lax.optimization_barrier((value, earlier))[0]

    def hop(block, k):
        pairs = [(a * inner + b, (a ^ k) * inner + b) for a in range(n_gx) for b in range(inner)]
        return lax.ppermute(block, "yz", pairs)

    def around(block, end=n_gx):
        return complete([block], end)

    def complete(held, end=n_gx):
        held = list(held)
        for m in range(len(held), end):
            low = m & -m
            block = held[m - low]
            held.append(hop(tie(block, held[1:m]) if m != low else block, low))
        return held

    def turn(picks):
        return [exchange(block, k) for k, block in enumerate(picks)]

    def exchange(block, k):
        if k == 0:
            return block
        return lax.ppermute(block, "gx", [(s, s ^ k) for s in range(n_gx)])

    def times(rows, other, which, weight, extra=None, far=False):
        if inner == 2:
            return product(which, rows, other, weight, extra, far)
        if extra is not None:
            weight = jnp.concatenate([weight, extra], axis=1)
        out = jnp.dot(other, weight, preferred_element_type=jnp.float32)
        out = out.reshape(n_gx, -1, weight.shape[1])
        return [out[0]] + [out[k].astype(jnp.bfloat16) for k in range(1, n_gx)]

    def partner(rows, joined):
        if inner == 2:
            if joined == 1:
                rows = [tie(rows[0], rows[1]), *rows[1:]]
            else:
                rows = [join(rows[i : i + joined]) for i in range(0, n_gx, joined)]
            return [lax.ppermute(block, "yz", swap) for block in rows]
        rows = jnp.concatenate(rows, axis=0)
        return lax.all_gather(rows, "yz", axis=1, tiled=True, axis_index_groups=groups)

    def give(partial):
        return [exchange(p, k) for k, p in enumerate(partial)]

    def collect(partial):
        total = partial[0]
        for p in partial[1:]:
            total = total + p.astype(jnp.float32)
        return total.astype(jnp.bfloat16)

    def pair_columns(part, r):
        if inner == 2:
            other = lax.ppermute(part, "yz", swap)
            return jnp.concatenate(
                [jnp.where(r == 0, part, other), jnp.where(r == 0, other, part)], axis=1
            )
        return lax.all_gather(part, "yz", axis=1, tiled=True, axis_index_groups=groups)

    def across(part):
        return [part] + [hop(part, k) for k in range(1, n_gx)]

    def body(tokens, gain, w_query, w_keyval, w_out, cache, lengths):
        gx = lax.axis_index("gx")
        yz = lax.axis_index("yz")
        z = yz // inner
        r = yz % inner
        _, span, width = tokens.shape
        features = width * n_yz
        pair_columns_here = inner * w_keyval.shape[1]
        ends = [span * sum(SHARES[: t + 1]) // sum(SHARES) for t in range(len(SHARES))]
        parts = [slice(start, end) for start, end in zip([0] + ends, ends)]
        length = lengths[0]

        first = around(tokens[0, parts[0]])

        values = tokens[0].astype(jnp.float32)
        mine = jnp.mean(values, axis=-1)
        moment = jnp.sum(jnp.square(values - mine[:, None]), axis=-1)
        stats = pair_columns(jnp.stack([mine, moment])[:, None], r)
        if inner == 2:
            w_keyval = w_keyval.T
            w_keyval = [w_keyval, lax.ppermute(w_keyval, "yz", swap)]
            stats = tie(stats, w_keyval)
        else:
            w_keyval = pair_columns(w_keyval, r)
        stats = jnp.concatenate(across(stats), axis=1)
        mean = jnp.mean(stats[0], axis=0)
        moments = jnp.sum(stats[1], axis=0) + width * jnp.sum(
            jnp.square(stats[0] - mean), axis=0
        )
        factor = lax.rsqrt(moments / features + 1e-06)
        gains = gain.reshape(n_gx, inner, width)[gx ^ jnp.arange(n_gx), r]
        which = r[None]
        info = jnp.stack([length, z])
        freq = jnp.exp(jnp.arange(HALF, dtype=jnp.float32) * (-2.0 * math.log(10000.0) / HEAD))
        positions = length + jnp.arange(span, dtype=jnp.int32)
        angles = positions.astype(jnp.float32)[:, None] * freq
        cosine = jnp.cos(angles)
        sine = jnp.sin(angles)

        index = z ^ gx ^ jnp.arange(n_gx, dtype=jnp.int32)
        order = [range(1, n_gx - 1), [n_gx - 1, 0]]
        shares = [
            (jnp.stack([z ^ gx ^ k for k in ks]), jnp.stack([gains[k] for k in ks])) for ks in order
        ]
        mean, factor, shares = tie(
            (mean[:, None], factor[:, None], shares), (cosine, sine, info, which, index)
        )

        def normalised(t, held, earlier=()):
            picks = {}
            for ks, (some, scale) in zip(order, shares):
                blocks = normalise(some, mean[parts[t]], factor[parts[t]], scale, held)
                picks.update(zip(ks, blocks))
                held = tie(held, (blocks, earlier))
            return [picks[k] for k in range(n_gx)]

        pairs = []

        def fresh(queries):
            return across(tail_sum(queries, pair_columns_here))

        picks = normalised(0, first)
        second = around(tie(tokens[0, parts[1]], picks[0]))
        rows = turn(picks)
        other = partner(rows, 1)
        partial = times(rows, other, which, w_query, w_keyval, True)
        queries = give(partial)
        pairs.append(fresh(queries))

        picks = normalised(1, tie(second, partial[0]), queries)
        past = lax.all_gather(tie(cache, picks[1]), "yz", axis=1, tiled=True)[0]
        rows = turn(picks)
        heads = attend(info, tie(queries, picks[0]), cosine, sine, past, pairs, True)
        first = around(heads)
        rows = tie(rows, heads)
        partial = times(rows, partner(rows, 2), which, w_query, w_keyval)
        queries = give(partial)
        pairs.append(fresh(queries))
        rows = turn(pick(index, tie(first, (queries[1:], pairs[1][1]))))
        heads = attend(info, queries, cosine, sine, past, pairs)
        second = around(heads, 3)

        partial = times(tie(rows, heads), partner(tie(rows, heads), 4), which, w_out)
        outs = [give(partial)]
        rows = turn(pick(index, complete(tie(second, partial[0]))))
        outs.append(give(times(rows, partner(tie(rows, outs[0][1:3]), 4), which, w_out)))
        outs = [collect(o) for o in outs]
        return jnp.concatenate(outs, axis=0)[None]

    return jax.shard_map(
        body,
        mesh=mesh,
        in_specs=(
            P("gx", None, "yz"),
            P(),
            P("gx", "yz"),
            P("gx", "yz"),
            P("gx", "yz"),
            P("gx", "yz", None),
            P("gx"),
        ),
        out_specs=P("gx", None, "yz"),
        check_vma=False,
    )
```
